256 devices in a mesh: layer: 16 (over y, z_hi, core), head: 4 (over x), dp: 4 (over z_lo).
Axes of the slice: x: 4, y: 4, z: 8 (z_hi: 2, z_lo: 4; z = z_hi * 4 + z_lo), core: 2. Of those that a mesh axis runs over, the one named last changes fastest.
Arguments:
- tokens: bfloat16 [4, 4096, 8192], P('dp', 'layer'), may hold values from -6 to 6
- lengths: int32 [4, 4096], P('dp', 'layer'), may hold values from 1 to 4096, as said below
- owner: int32 [1], replicated, may hold values from 0 to 79
- wq_slabs: bfloat16 [16, 8192, 4096], P('layer', 'dp', 'head'), may hold values from -0.0625 to 0.0625
- wkv_slabs: bfloat16 [16, 8192, 4, 256], P('layer', 'dp', 'head'), may hold values from -0.0625 to 0.0625
- cache_keys: bfloat16 [4, 4096, 512], P('dp', None, 'head'), may hold values from -1000 to 1000
- resident_value_cache: bfloat16 [4, 4096, 512], P('dp', None, 'head'), may hold values from -6 to 6
Outputs:
- attended: bfloat16 [4, 4096, 4096], P('dp', 'layer', 'head')
The draws below stay inside these ranges and needn't reach their ends.
Inputs may be any that keep to these rules, and one draw needn't show every extreme that they name: `lengths`: every group has a row of length 4096.
All inputs are finite; a program needn't handle non-finite values.
Results may differ from the reference program's by a relative error of at most 0.015.
The reference program's roundings to bfloat16 on the way count: a program that leaves them out, or rounds other values in their place, can miss the bound.
Values may be sent and summed in bfloat16 or wider, within the bound.
No kernel may reach another device: no remote copies, remote signals or barrier semaphores. Data moves between devices by JAX's collectives and lax.ppermute only.
A program may use at most 128 MiB of HBM per device.

```python
import math
import jax
import jax.numpy as jnp
from jax import lax

D = 8192
QH = 32
KVH = 4
HD = 128
LAYERS = 80
CTX = 4096
GROUPS = 4
GROUP_ROWS = 4096
QW = 4096
KVW = 512
N_LAYER = 16


def draw_lengths(key, part):
    key = jax.random.fold_in(key, 5)
    first, second = jax.random.split(key)
    spans = jax.random.randint(first, (GROUPS, GROUP_ROWS), 1, CTX + 1)
    chosen = jax.random.randint(second, (GROUPS, 1), 0, GROUP_ROWS)
    rows_index = jnp.arange(GROUP_ROWS)[None, :]
    return jnp.where(rows_index == chosen, CTX, spans).astype(jnp.int32)


def draw_cache_keys(key, part):
    key = jax.random.fold_in(key, 7)
    first = jax.random.fold_in(key, 0)
    base = jnp.clip(jax.random.normal(first, (GROUPS, CTX, KVW), jnp.float32), -6.0, 6.0)
    return base.astype(jnp.bfloat16)


def block_scale(key, extent, pieces, smallest, top_value):
    loudness = 1.0
    for axis_at, blocks in pieces:
        draws = jax.random.uniform(jax.random.fold_in(jax.random.fold_in(key, 6), axis_at), (blocks,), jnp.float32, smallest / len(pieces), top_value / len(pieces))
        loudness = loudness * jnp.repeat(jnp.exp(draws), extent[axis_at] // blocks).reshape((-1,) + (1,) * (len(extent) - 1 - axis_at))
    return loudness


def noise(rng, shape, scale, limit, cuts=(), held_as=jnp.bfloat16):
    entries = jax.random.normal(rng, shape, jnp.float32) * scale
    if len(cuts) > 0:
        entries = block_scale(rng, shape, cuts, -0.22, 0.18) * entries
    return jnp.clip(entries, min=-limit, max=limit).astype(held_as)


def setup_inputs(seed: int = 0) -> dict:
    arg_keys = jax.random.split(jax.random.key(seed), 8)
    tokens = noise(arg_keys[0], (GROUPS, GROUP_ROWS, D), 1.0, 6.0, ((0, 4), (1, 16)))
    lengths = draw_lengths(jax.random.fold_in(arg_keys[7], 71), 0)
    owner = jax.random.randint(arg_keys[2], (1,), 0, LAYERS).astype(jnp.int32)
    wq_slabs = noise(arg_keys[3], (N_LAYER, D, QW), D ** -0.5, 0.0625, ((0, 16), (1, 4), (2, 4)))
    wkv_slabs = noise(arg_keys[4], (N_LAYER, D, KVH, 2 * HD), D ** -0.5, 0.0625, ((0, 16), (1, 4), (2, 4)))
    cache_keys = draw_cache_keys(jax.random.fold_in(arg_keys[7], 71), 0)
    resident_value_cache = noise(arg_keys[6], (GROUPS, CTX, KVW), 1.0, 6.0, ((0, 4), (2, 4)))
    return dict(tokens=tokens, lengths=lengths, owner=owner, wq_slabs=wq_slabs, wkv_slabs=wkv_slabs, cache_keys=cache_keys, resident_value_cache=resident_value_cache)


rope_base = 500000.0

def rotary(vectors, places):
    half_dim = vectors.shape[-1] // 2
    channel = jnp.arange(half_dim).astype(jnp.float32)
    rates = jnp.power(jnp.float32(rope_base), -2.0 * channel / vectors.shape[-1])
    angles = places[..., None] * rates
    cosine = jnp.cos(angles)
    sine = jnp.sin(angles)
    first = vectors[..., :half_dim]
    second = vectors[..., half_dim:]
    return jnp.concatenate([first * cosine - second * sine, second * cosine + first * sine], -1)

def attend(query_rows, fresh_key_rows, fresh_value_rows, keys, values, lens):
    score_scale = 1.0 / math.sqrt(query_rows.shape[-1])
    scores = jnp.einsum('bkgd,ckd->bkgc', query_rows.astype(jnp.float32), keys.astype(jnp.float32)) * score_scale
    self_token_score = jnp.einsum('ijcr,ijr->ijc', query_rows.astype(jnp.float32), fresh_key_rows.astype(jnp.float32)) * score_scale
    visible = (jnp.arange(keys.shape[0]).astype(jnp.int32)[None, :] < lens[:, None])[:, None, None, :]
    peak = jnp.maximum(lax.optimization_barrier(jnp.max(jnp.where(visible, scores, -jnp.inf), -1)), self_token_score)
    weights = jnp.where(visible, jnp.exp(scores - peak[..., None]), 0.0)
    own_weight = jnp.exp(self_token_score - peak)
    total = lax.optimization_barrier(jnp.sum(weights, -1)) + own_weight
    weights_low = weights.astype(jnp.bfloat16)
    own_low = own_weight.astype(jnp.bfloat16)
    mixed = jnp.einsum('bkgc,ckd->bkgd', weights_low.astype(jnp.float32), values.astype(jnp.float32))
    mixed = mixed + own_low.astype(jnp.float32)[..., None] * fresh_value_rows.astype(jnp.float32)[:, :, None, :]
    return (mixed / total[..., None]).astype(jnp.bfloat16)

def reference(tokens, lengths, owner, wq_slabs, wkv_slabs, cache_keys, resident_value_cache):
    holder = (owner[0] % N_LAYER).astype(jnp.int32)
    current_wq = lax.dynamic_index_in_dim(wq_slabs, holder, 0, keepdims=False)
    current_wkv = lax.dynamic_index_in_dim(wkv_slabs, holder, 0, keepdims=False).reshape(D, KVH * 2 * HD)
    heads_per_group = QH // KVH
    block = math.gcd(GROUP_ROWS, 256)
    count = GROUP_ROWS // block

    def one_group(inputs):
        rows, lens, group_keys, group_values = inputs
        query_raw = jnp.dot(rows, current_wq, preferred_element_type=jnp.float32).reshape(GROUP_ROWS, KVH, heads_per_group, HD)
        kv_raw = jnp.dot(rows, current_wkv, preferred_element_type=jnp.float32).reshape(GROUP_ROWS, KVH, 2 * HD)
        places = lens.astype(jnp.float32)
        query_rows = rotary(query_raw, places[:, None, None]).astype(jnp.bfloat16)
        fresh_key_rows = rotary(kv_raw[..., :HD], places[:, None]).astype(jnp.bfloat16)
        fresh_value_rows = kv_raw[..., HD:].astype(jnp.bfloat16)
        keys = group_keys.reshape(CTX, KVH, HD)
        values = group_values.reshape(CTX, KVH, HD)

        def one_block(parts):
            return attend(parts[0], parts[1], parts[2], keys, values, parts[3])
        result = lax.map(one_block, (query_rows.reshape(count, block, KVH, heads_per_group, HD), fresh_key_rows.reshape(count, block, KVH, HD), fresh_value_rows.reshape(count, block, KVH, HD), lens.reshape(count, block)))
        return result.reshape(GROUP_ROWS, QW)
    return lax.map(one_group, (tokens, lengths, cache_keys, resident_value_cache))
```

```python
import functools
import math

import jax
import jax.numpy as jnp
from jax import lax
from jax.experimental import pallas as pl
from jax.experimental.pallas import tpu as pltpu
from jax.sharding import PartitionSpec as P

rope_base = 500000.0
AXES = ("layer", "head", "dp")
NY, NZH, NCO, NX, NZL = 4, 2, 2, 4, 4
NZ = NZH * NZL


def linear(y, z, co, x):
    y, z, x = y % NY, z % NZ, x % NX
    return (((y * NZH + z // NZL) * NCO + co) * NX + x) * NZL + z % NZL


def moves(to):
    pairs = []
    for y in range(NY):
        for z in range(NZ):
            for co in range(NCO):
                for x in range(NX):
                    pairs.append((linear(y, z, co, x), linear(*to(y, z, co, x))))
    return pairs


def send(block, to):
    return lax.ppermute(block, AXES, moves(to))


def y_step(n):
    return lambda y, z, co, x: (y + n, z, co, x)


def z_step(n):
    return lambda y, z, co, x: (y, z + n, co, x)


def other_core(y, z, co, x):
    return (y, z, 1 - co, x)


def z_mirror(y, z, co, x):
    return (y, NZ - 1 - z, co, x)


class Piece:
    def __init__(self, block, segs):
        self.block = block
        self.segs = segs

    def rows(self, lo, hi):
        out, at = [], 0
        for zo, yo, first, n in self.segs:
            a, b = max(lo, at), min(hi, at + n)
            if a < b:
                out.append((zo, yo, first + a - at, b - a))
            at += n
        return Piece(self.block[lo:hi], out)

    def hop_y(self, n):
        return Piece(send(self.block, y_step(n)), [(zo, (yo - n) % NY, f, r) for zo, yo, f, r in self.segs])

    def hop_z(self, n):
        return Piece(send(self.block, z_step(n)), [((zo - n) % NZ, yo, f, r) for zo, yo, f, r in self.segs])


def join(pieces):
    return Piece(jnp.concatenate([p.block for p in pieces], 0), [s for p in pieces for s in p.segs])


def ring_y(own):
    half = own.block.shape[0] // 2
    up, down = own.hop_y(1), own.hop_y(-1)
    return [own, up, down, up.rows(0, half).hop_y(1), down.rows(half, 2 * half).hop_y(-1)]


def ring_z(own):
    half = own.block.shape[0] // 2
    got, up, down = [own], own, own
    for _ in range(NZ // 2 - 1):
        up, down = up.hop_z(1), down.hop_z(-1)
        got += [up, down]
    return got + [up.rows(0, half).hop_z(1), down.rows(half, 2 * half).hop_z(-1)]


def project_kernel(segs, chunk, place_ref, mine_ref, partner_ref, cos_ref, sin_ref, *rest):
    weights, out_ref, acc = rest[:-2], rest[-2], rest[-1]
    rows = mine_ref.shape[0]
    acc[...] = jnp.zeros_like(acc)
    for w_ref, w_segs in zip(weights, segs):
        at = 0
        for zo, yo, first, n in w_segs:
            start = pl.multiple_of(place_ref[zo * NY + yo] * chunk + first, 128)
            w = w_ref[at : at + n, :]
            acc[:rows, :] += jnp.dot(mine_ref[:, pl.ds(start, n)], w, preferred_element_type=jnp.float32)
            acc[rows:, :] += jnp.dot(partner_ref[:, pl.ds(start, n)], w, preferred_element_type=jnp.float32)
            at += n
    for h in range(out_ref.shape[1] // 128):
        x = acc[:, h * 128 : (h + 1) * 128]
        t = 0 if h == 0 else 1
        out = x * cos_ref[t] + pltpu.roll(x, 64, 1) * sin_ref[t]
        out_ref[:, h * 128 : (h + 1) * 128] = out.astype(jnp.bfloat16)


def project(pieces, place, mine, partner, cosine, sine):
    rows, depth = mine.shape
    cols = pieces[0].block.shape[1]
    vmem = pl.BlockSpec(memory_space=pltpu.VMEM)
    return pl.pallas_call(
        functools.partial(project_kernel, [p.segs for p in pieces], depth // (NY * NZ)),
        out_shape=jax.ShapeDtypeStruct((2 * rows, cols), jnp.bfloat16),
        in_specs=[pl.BlockSpec(memory_space=pltpu.SMEM)] + [vmem] * (4 + len(pieces)),
        out_specs=vmem,
        scratch_shapes=[pltpu.VMEM((2 * rows, cols), jnp.float32)],
        compiler_params=pltpu.CompilerParams(vmem_limit_bytes=48 * 2**20),
        cost_estimate=pl.CostEstimate(
            flops=4 * rows * depth * cols, bytes_accessed=4 * rows * depth + 2 * depth * cols, transcendentals=0
        ),
    )(place, mine, partner, cosine, sine, *[p.block for p in pieces])


def rope_tables(places, head_dim):
    channel = jnp.arange(head_dim // 2).astype(jnp.float32)
    rates = jnp.power(jnp.float32(rope_base), -2.0 * channel / head_dim)
    angles = places[:, None] * rates
    cosine, sine = jnp.cos(angles), jnp.sin(angles)
    return jnp.concatenate([cosine, cosine], -1), jnp.concatenate([-sine, sine], -1)


def attend(query_rows, fresh_key_rows, fresh_value_rows, keys, values, lens):
    score_scale = 1.0 / math.sqrt(query_rows.shape[-1])
    scores = (
        jnp.einsum("bkgd,ckd->bkgc", query_rows, keys, preferred_element_type=jnp.float32)
        * score_scale
    )
    self_token_score = (
        jnp.einsum("ijcr,ijr->ijc", query_rows, fresh_key_rows, preferred_element_type=jnp.float32)
        * score_scale
    )
    visible = (jnp.arange(keys.shape[0])[None, :] < lens[:, None])[:, None, None, :]
    peak = jnp.maximum(jnp.max(jnp.where(visible, scores, -jnp.inf), -1), self_token_score)
    weights = jnp.where(visible, jnp.exp(scores - peak[..., None]), 0.0)
    own_weight = jnp.exp(self_token_score - peak)
    total = jnp.sum(weights, -1) + own_weight
    weights_low = weights.astype(jnp.bfloat16)
    own_low = own_weight.astype(jnp.bfloat16)
    mixed = jnp.einsum("bkgc,ckd->bkgd", weights_low, values, preferred_element_type=jnp.float32)
    mixed = (
        mixed
        + own_low.astype(jnp.float32)[..., None]
        * fresh_value_rows.astype(jnp.float32)[:, :, None, :]
    )
    return (mixed / total[..., None]).astype(jnp.bfloat16)


def local(tokens, lengths, owner, wq_slabs, wkv_slabs, cache_keys, resident_value_cache):
    mine = tokens[0]
    lens = lengths[0]
    rows, depth = mine.shape
    head_dim = cache_keys.shape[2]
    part = wq_slabs.shape[1]
    layer, zl = lax.axis_index("layer"), lax.axis_index("dp")
    y, zh, co = layer // 4, layer // 2 % 2, layer % 2
    holder = owner[0] % lax.axis_size("layer")
    y0, zh0, co0 = holder // 4, holder // 2 % 2, holder % 2

    partner = send(mine, other_core)
    partner_lens = send(lengths, other_core)[0]
    cos_rows, sin_rows = rope_tables(jnp.concatenate([lens, partner_lens]).astype(jnp.float32), head_dim)
    cosine = jnp.stack([jnp.where(co == 0, cos_rows, 1.0), cos_rows])
    sine = jnp.stack([jnp.where(co == 0, sin_rows, 0.0), sin_rows])

    wq, wkv = wq_slabs[0], wkv_slabs[0, :, 0]
    half_q = wq.shape[1] // 2
    low = jnp.concatenate([wkv[:, :head_dim], wq[:, :half_q]], 1)
    high = jnp.concatenate([wkv[:, head_dim:], wq[:, half_q:]], 1)
    from_core = send(jnp.where(co == 0, high, low), other_core)
    slab = jnp.where(co == co0, jnp.where(co == 0, low, high), from_core)

    fourth = part // NY
    rel = (y - y0) % NY
    up = send(slab[fourth : fourth * 5 // 2], y_step(1))
    down = send(slab[fourth * 5 // 2 :], y_step(-1))
    far = jnp.concatenate(
        [send(up[fourth:], y_step(1)), send(down[: fourth // 2], y_step(-1))], 0
    )
    got = jnp.where(
        rel == 0, slab[:fourth], jnp.where(rel == 1, up[:fourth], jnp.where(rel == 2, far, down[fourth // 2 :]))
    )
    chunk = fourth // 2
    mirrored = send(got[chunk:], z_mirror)
    own = jnp.where(zh == zh0, got[:chunk], mirrored)

    zs = (zh * NZL + zl + jnp.arange(NZ)) % NZ
    z_is_home = zs // NZL == zh0
    quarter = jnp.where(z_is_home, zs % NZL, NZL - 1 - zs % NZL)
    rels = (rel + jnp.arange(NY)) % NY
    place = (quarter[:, None] * NY + rels[None, :]) * 2 + jnp.where(z_is_home, 0, 1)[:, None]
    place = place.reshape(-1).astype(jnp.int32)

    seg = [(0, 0, 0, chunk)]
    cut = 3 * head_dim
    part_b, part_a = Piece(own[:, :cut], seg), Piece(own[:, cut:], seg)
    got_a = ring_z(join(ring_y(part_a)))
    z_b = ring_z(part_b)
    got_b = ring_y(join(z_b[:3])) + ring_y(join(z_b[3:]))

    out_b = project(got_b, place, mine, partner, cosine, sine)
    out_a = project(got_a, place, mine, partner, cosine[1:][jnp.array([0, 0])], sine[1:][jnp.array([0, 0])])
    mine_b, mine_a = out_b[:rows], out_a[:rows]
    theirs_b, theirs_a = send(out_b[rows:], other_core), send(out_a[rows:], other_core)

    first = co == 0
    fresh_keys = jnp.where(first, mine_b[:, :head_dim], theirs_b[:, :head_dim])
    fresh_values = jnp.where(first, theirs_b[:, :head_dim], mine_b[:, :head_dim])
    q_mine = jnp.concatenate([mine_b[:, head_dim:], mine_a], 1)
    q_theirs = jnp.concatenate([theirs_b[:, head_dim:], theirs_a], 1)
    queries = jnp.where(first, jnp.concatenate([q_mine, q_theirs], 1), jnp.concatenate([q_theirs, q_mine], 1))
    heads = queries.shape[1] // head_dim

    keys, values = cache_keys[0][:, None, :], resident_value_cache[0][:, None, :]
    block = math.gcd(rows, 64)
    count = rows // block

    def one_block(parts):
        return attend(parts[0], parts[1], parts[2], keys, values, parts[3])

    result = lax.map(
        one_block,
        (
            queries.reshape(count, block, 1, heads, head_dim),
            fresh_keys.reshape(count, block, 1, head_dim),
            fresh_values.reshape(count, block, 1, head_dim),
            lens.reshape(count, block),
        ),
    )
    return result.reshape(1, rows, heads * head_dim)


def solution(mesh):
    return jax.shard_map(
        local,
        mesh=mesh,
        in_specs=(
            P("dp", "layer", None),
            P("dp", "layer"),
            P(),
            P("layer", "dp", "head"),
            P("layer", "dp", "head", None),
            P("dp", None, "head"),
            P("dp", None, "head"),
        ),
        out_specs=P("dp", "layer", "head"),
        check_vma=False,
    )
```

```python
import functools
import math

import jax
import jax.numpy as jnp
from jax import lax
from jax.experimental import pallas as pl
from jax.experimental.pallas import tpu as pltpu
from jax.sharding import Mesh, PartitionSpec as P

rope_base = 500000.0
AXES = ("y", "z_hi", "core", "head", "dp")
NY, NZH, NCO, NX, NZL = 4, 2, 2, 4, 4
NZ = NZH * NZL
VMEM = pl.BlockSpec(memory_space=pltpu.VMEM)
SMEM = pl.BlockSpec(memory_space=pltpu.SMEM)
ANY = pl.BlockSpec(memory_space=pl.ANY)
EARLY_CHUNKS = (0, 1, 2, 3, 4, 5, 6, 8, 9, 10)
LATE_CHUNKS = (7, 11, 12, 13, 14, 15)


def linear(y, z, co, x):
    y, z, x = y % NY, z % NZ, x % NX
    return (((y * NZH + z // NZL) * NCO + co) * NX + x) * NZL + z % NZL


def moves(to):
    pairs = []
    for y in range(NY):
        for z in range(NZ):
            for co in range(NCO):
                for x in range(NX):
                    pairs.append((linear(y, z, co, x), linear(*to(y, z, co, x))))
    return pairs


def send(block, to):
    return lax.ppermute(block, AXES, moves(to))


def y_step(n):
    return lambda y, z, co, x: (y + n, z, co, x)


def z_step(n):
    return lambda y, z, co, x: (y, z + n, co, x)


def x_step(n):
    return lambda y, z, co, x: (y, z, co, x + n)


def other_core(y, z, co, x):
    return (y, z, 1 - co, x)


def z_pair(y, z, co, x):
    return (y, z ^ 1, co, x)


def z_pair_other_core(y, z, co, x):
    return (y, z ^ 1, 1 - co, x)


def z_mirror(y, z, co, x):
    return (y, NZ - 1 - z, co, x)


def after(block, *others):
    return lax.optimization_barrier((block,) + others)[0]


def run_all(copies):
    for copy in copies:
        copy.start()
    for copy in copies:
        copy.wait()


def pack_kernel(main, fifth, dim, core_ref, wq_ref, wkv_ref, out_ref, sems):
    core = core_ref[0]
    copies = []
    for piece in range(NY):
        for half in range(2):
            base = (piece * 2 + half) * (main + fifth)
            first_row = piece * main
            column = pl.multiple_of(half * 4 * dim + core * 2 * dim, dim)
            copies.append((wq_ref.at[first_row : first_row + main, pl.ds(column, 2 * dim)], out_ref.at[base : base + main, :]))
            for side in range(2):
                row = pl.multiple_of(first_row + core * 2 * fifth + side * fifth, fifth)
                copies.append(
                    (
                        wkv_ref.at[pl.ds(row, fifth), half * dim : (half + 1) * dim],
                        out_ref.at[base + main : base + main + fifth, side * dim : (side + 1) * dim],
                    )
                )
    run_all([pltpu.make_async_copy(src, dst, sems.at[i]) for i, (src, dst) in enumerate(copies)])


def pack(core, wq, wkv, main, fifth, dim):
    return pl.pallas_call(
        functools.partial(pack_kernel, main, fifth, dim),
        out_shape=jax.ShapeDtypeStruct((NY * 2 * (main + fifth), 2 * dim), wq.dtype),
        in_specs=[SMEM, ANY, ANY],
        out_specs=VMEM,
        scratch_shapes=[pltpu.SemaphoreType.DMA((NY * 6,))],
        compiler_params=pltpu.CompilerParams(vmem_limit_bytes=60 * 2**20),
        cost_estimate=pl.CostEstimate(flops=0, bytes_accessed=5 * 2**20, transcendentals=0),
    )(core.reshape(1), wq, wkv)


def order_kernel(wide, place_ref, slot_ref, mine_ref, same_ref, up_ref, down_ref, far_up_ref, far_down_ref, early_ref, late_ref, sems):
    rows = mine_ref.shape[0]
    per_quarter = same_ref.shape[1] // wide
    half = rows // 2
    held = [(same_ref, 0, 0, rows), (up_ref, 1, 0, rows), (down_ref, 2, 0, rows)]
    held += [(far_up_ref, 3, 0, half), (far_down_ref, 3, half, half)]
    at = 0
    for out_ref, chunks in ((early_ref, EARLY_CHUNKS), (late_ref, LATE_CHUNKS)):
        for i, chunk in enumerate(chunks):
            place = place_ref[chunk]
            column = pl.multiple_of(place * wide, wide)
            pltpu.make_async_copy(mine_ref.at[:, pl.ds(column, wide)], out_ref.at[i, :rows, :], sems.at[at]).start()
            at += 1
            inner = pl.multiple_of(place % per_quarter * wide, wide)
            for ref, slot, first, n in held:

                @pl.when(slot_ref[chunk] == slot)
                def _(ref=ref, first=first, n=n, inner=inner, out_ref=out_ref, i=i, sem=at + (first > 0)):
                    pltpu.make_async_copy(
                        ref.at[:, pl.ds(inner, wide)], out_ref.at[i, rows + first : rows + first + n, :], sems.at[sem]
                    ).start()

            at += 2
    at = 0
    for out_ref, chunks in ((early_ref, EARLY_CHUNKS), (late_ref, LATE_CHUNKS)):
        for i, chunk in enumerate(chunks):
            block = out_ref.at[i, :rows, :]
            pltpu.make_async_copy(block, block, sems.at[at]).wait()
            for ref, slot, first, n in held:

                @pl.when(slot_ref[chunk] == slot)
                def _(first=first, n=n, out_ref=out_ref, i=i, sem=at + 1 + (first > 0)):
                    block = out_ref.at[i, rows + first : rows + first + n, :]
                    pltpu.make_async_copy(block, block, sems.at[sem]).wait()

            at += 3


def order_tokens(place, slot, wide, mine, pieces):
    rows, depth = mine.shape
    return pl.pallas_call(
        functools.partial(order_kernel, wide),
        out_shape=[
            jax.ShapeDtypeStruct((len(chunks), 2 * rows, wide), mine.dtype) for chunks in (EARLY_CHUNKS, LATE_CHUNKS)
        ],
        in_specs=[SMEM, SMEM] + [ANY] * 6,
        out_specs=[VMEM, VMEM],
        scratch_shapes=[pltpu.SemaphoreType.DMA((3 * NY * NZL,))],
        compiler_params=pltpu.CompilerParams(vmem_limit_bytes=20 * 2**20),
        cost_estimate=pl.CostEstimate(flops=0, bytes_accessed=8 * rows * depth, transcendentals=0),
    )(place, slot, mine, *pieces)


def project_kernel(parts, main, first, last, core_ref, tokens_ref, others_ref, *rest):
    rest = list(rest)
    start_ref = None if first else rest.pop(0)
    cos_ref, sin_ref = (rest.pop(0), rest.pop(0)) if last else (None, None)
    weights, out_ref = rest[: len(parts)], rest[len(parts)]
    acc = rest[len(parts) + 1] if last else out_ref
    two = weights[0].shape[1]
    dim = two // 2
    core = core_ref[0]
    rows = tokens_ref.shape[1]
    acc[...] = jnp.zeros_like(acc) if first else start_ref[...]
    column = pl.multiple_of(core * (main // 2), main // 2)
    for w_ref, part in zip(weights, parts):
        at = 0
        for chunk, begin, n in part:
            i = (LATE_CHUNKS if last else EARLY_CHUNKS).index(chunk)
            end = min(begin + n, main)
            for side, ref in enumerate((tokens_ref, others_ref)):
                cut = slice(side * rows, (side + 1) * rows)
                acc[cut, :two] += jnp.dot(
                    ref[i, :, begin:end], w_ref[at : at + end - begin, :], preferred_element_type=jnp.float32
                )
                if begin + n > main:
                    low = at + main - begin
                    packed = w_ref[low : low + main // 4, :]
                    w = jnp.concatenate([packed[:, :dim], packed[:, dim:]], 0)
                    acc[cut, two:] += jnp.dot(
                        ref[i, :, pl.ds(column, main // 2)], w, preferred_element_type=jnp.float32
                    )
            at += n
    if last:
        for h in range(2):
            x = acc[:, h * dim : (h + 1) * dim]
            out = x * cos_ref[...] + pltpu.roll(x, dim // 2, 1) * sin_ref[...]
            out_ref[:, h * dim : (h + 1) * dim] = out.astype(jnp.bfloat16)
        x = acc[:, two:]
        high = x.astype(jnp.bfloat16)
        out_ref[:, two : two + dim] = high
        out_ref[:, two + dim :] = (x - high.astype(jnp.float32)).astype(jnp.bfloat16)


def project(core, tokens, others, weights, parts, main, start, tables):
    rows = 2 * tokens.shape[1]
    cols = weights[0].shape[1]
    first, last = start is None, tables is not None
    extra = ([] if first else [start]) + (list(tables) if last else [])
    taken = sum(w.shape[0] for w in weights)
    acc_shape = (rows, cols + cols // 2)
    return pl.pallas_call(
        functools.partial(project_kernel, parts, main, first, last),
        out_shape=jax.ShapeDtypeStruct((rows, 2 * cols), jnp.bfloat16)
        if last
        else jax.ShapeDtypeStruct(acc_shape, jnp.float32),
        in_specs=[SMEM] + [VMEM] * (2 + len(extra) + len(weights)),
        out_specs=VMEM,
        scratch_shapes=[pltpu.VMEM(acc_shape, jnp.float32)] if last else [],
        compiler_params=pltpu.CompilerParams(vmem_limit_bytes=22 * 2**20),
        cost_estimate=pl.CostEstimate(
            flops=2 * rows * taken * cols, bytes_accessed=2 * taken * (rows + cols), transcendentals=0
        ),
    )(core.reshape(1), tokens, others, *extra, *weights)


def rope_tables(places, head_dim):
    channel = jnp.arange(head_dim // 2).astype(jnp.float32)
    rates = jnp.power(jnp.float32(rope_base), -2.0 * channel / head_dim)
    angles = places[:, None] * rates
    cosine, sine = jnp.cos(angles), jnp.sin(angles)
    return jnp.concatenate([cosine, cosine], -1), jnp.concatenate([-sine, sine], -1)


def sort_rows(perm_ref, x):
    return jnp.dot(perm_ref[...], x, preferred_element_type=jnp.float32).astype(jnp.bfloat16)


def over_cache(block, key_block, bounds_ref, lens_ref, kt_ref, v_ref, qs, scores, put):
    heads, rows, dim = qs.shape
    m_rows = heads * block
    scale = jnp.float32(math.log2(math.e) / math.sqrt(dim))
    tiles = key_block // dim
    count = rows // block

    def score(b, j, peak):
        off = pl.multiple_of(j * key_block, key_block)
        q = qs[:, b * block : (b + 1) * block, :].reshape(m_rows, dim)
        left = lens_ref[b * block : (b + 1) * block, :] - off
        lane = lax.broadcasted_iota(jnp.int32, (block, dim), 1)
        s = jnp.dot(q, kt_ref[:, pl.ds(off, key_block)], preferred_element_type=jnp.float32)
        for t in range(tiles):
            seen = lane < left - t * dim
            tile = jnp.concatenate(
                [
                    jnp.where(seen, s[h * block : (h + 1) * block, t * dim : (t + 1) * dim], -1e30)
                    for h in range(heads)
                ],
                0,
            )
            scores[b % 2, :, pl.ds(off + t * dim, dim)] = tile
            peak = jnp.maximum(peak, tile)
        return peak

    def mix(b, j, shift, sums):
        total, mixed = sums
        off = pl.multiple_of(j * key_block, key_block)
        low_bits = []
        for t in range(tiles):
            w = jnp.exp2(scores[b % 2, :, pl.ds(off + t * dim, dim)] * scale - shift)
            total = total + w
            low_bits.append(w.astype(jnp.bfloat16))
        mixed = mixed + jnp.dot(
            jnp.concatenate(low_bits, 1), v_ref[pl.ds(off, key_block), :], preferred_element_type=jnp.float32
        )
        return total, mixed

    zero = jnp.zeros((m_rows, dim), jnp.float32)
    lowest = jnp.full((m_rows, dim), -1e30, jnp.float32)
    peak, shift, before = None, None, 0
    for b in range(count + 1):
        now = bounds_ref[b] if b < count else 0
        peak_next, sums = lowest, (zero, zero)
        if b == 0:
            peak_next = lax.fori_loop(0, now, lambda j, p: score(0, j, p), peak_next)
        elif b < count:

            def step(j, carry, b=b, shift=shift):
                return score(b, j, carry[0]), mix(b - 1, j, shift, carry[1])

            peak_next, sums = lax.fori_loop(0, before, step, (peak_next, sums))
            peak_next = lax.fori_loop(before, now, lambda j, p, b=b: score(b, j, p), peak_next)
        else:
            sums = lax.fori_loop(0, before, lambda j, s, b=b, shift=shift: mix(b - 1, j, shift, s), sums)
        if b > 0:
            total = jnp.broadcast_to(jnp.sum(sums[0], -1, keepdims=True), (m_rows, dim))
            put((b - 1) * block, peak, total, sums[1])
        if b < count:
            peak = jnp.broadcast_to(jnp.max(peak_next, -1, keepdims=True), (m_rows, dim))
            shift = peak * scale
        before = now


def keep(refs, heads, block):
    def put(r0, *values):
        for ref, value in zip(refs, values):
            ref[:, r0 : r0 + block, :] = value.reshape(heads, block, value.shape[1])

    return put


def early_kernel(block, key_block, bounds_ref, a_ref, b_ref, perm_ref, lens_ref, kt_ref, v_ref, *rest):
    outs, scores = rest[:4], rest[4]
    qs = outs[0]
    dim = qs.shape[2]
    for i, ref in enumerate((a_ref, b_ref)):
        for h in range(2):
            qs[2 * i + h] = sort_rows(perm_ref, ref[:, h * dim : (h + 1) * dim])
    put = keep(outs[1:], 4, block)
    over_cache(block, key_block, bounds_ref, lens_ref, kt_ref, v_ref, qs, scores, put)


def late_kernel(block, key_block, half_ref, column_ref, bounds_ref, *rest):
    parts, early, rest = rest[:4], rest[4:8], rest[8:]
    cos_ref, sin_ref, perm_ref, back_ref, lens_ref, kt_ref, v_ref, out_ref, qs, scores, fresh, result = rest
    dim = qs.shape[2]
    scale = jnp.float32(math.log2(math.e) / math.sqrt(dim))
    for i, ref in enumerate(parts[2:]):
        for h in range(2):
            qs[2 * i + h] = sort_rows(perm_ref, ref[:, h * dim : (h + 1) * dim])
    sums = [
        sum(ref[:, c : c + dim].astype(jnp.float32) for c in range(2 * dim, ref.shape[1], dim)) for ref in parts
    ]
    near, far = sums[0] + sums[1], sums[2] + sums[3]
    first = half_ref[0] == 0
    key = jnp.where(first, near, far)
    key = key * cos_ref[...] + pltpu.roll(key, dim // 2, 1) * sin_ref[...]
    fresh[0] = sort_rows(perm_ref, key.astype(jnp.bfloat16)).astype(jnp.float32)
    fresh[1] = sort_rows(perm_ref, jnp.where(first, far, near).astype(jnp.bfloat16)).astype(jnp.float32)

    def finish(q, cut, peak, total, mixed):
        own = jnp.sum(q.astype(jnp.float32) * fresh[0, cut, :], -1, keepdims=True)
        top = jnp.maximum(peak, own)
        shrink = jnp.exp2((peak - top) * scale)
        own_weight = jnp.exp2((own - top) * scale)
        low = own_weight.astype(jnp.bfloat16).astype(jnp.float32)
        value = mixed * shrink + low * fresh[1, cut, :]
        return (value / (total * shrink + own_weight)).astype(jnp.bfloat16)

    def put(r0, peak, total, mixed):
        cut = slice(r0, r0 + block)
        for h in range(4):
            at = slice(h * block, (h + 1) * block)
            result[4 + h, cut, :] = finish(qs[h, cut, :], cut, peak[at], total[at], mixed[at])
            result[h, cut, :] = finish(*[early[0][h, cut, :], cut] + [ref[h, cut, :] for ref in early[1:]])

    over_cache(block, key_block, bounds_ref, lens_ref, kt_ref, v_ref, qs, scores, put)
    for i in range(4):
        for h in range(2):
            column = pl.multiple_of((column_ref[i] + h) * dim, dim)
            rows_back = jnp.dot(back_ref[...], result[2 * i + h], preferred_element_type=jnp.float32)
            out_ref[:, pl.ds(column, dim)] = rows_back.astype(jnp.bfloat16)


def attention_call(kernel, out_shape, scratch, smem, args, rows, context, dim):
    heads = 4
    many = isinstance(out_shape, list)
    return pl.pallas_call(
        kernel,
        out_shape=out_shape,
        in_specs=[SMEM] * smem + [VMEM] * (len(args) - smem),
        out_specs=[VMEM] * len(out_shape) if many else VMEM,
        scratch_shapes=scratch,
        compiler_params=pltpu.CompilerParams(vmem_limit_bytes=30 * 2**20),
        cost_estimate=pl.CostEstimate(
            flops=4 * heads * rows * context * dim,
            bytes_accessed=4 * context * dim,
            transcendentals=heads * rows * context,
        ),
    )(*args)


def local(tokens, lengths, owner, wq_slabs, wkv_slabs, cache_keys, resident_value_cache):
    mine = tokens[0]
    lens = lengths[0]
    rows, depth = mine.shape
    dim = cache_keys.shape[2]
    part = wq_slabs.shape[1]
    y, zh, co, x, zl = (lax.axis_index(name) for name in AXES)
    z = zh * NZL + zl
    holder = owner[0] % (NY * NZH * NCO)
    y0, zh0, co0 = holder // (NZH * NCO), holder // NCO % NZH, holder % NCO
    main = part // NY
    fifth = main // 4
    chunk = main + fifth
    cut = main * 3 // 4

    wq, wkv = wq_slabs[0], wkv_slabs[0, :, 0]
    from_core = send(pack(1 - co, wq, wkv, main, fifth, dim), other_core)
    held = pack(co, wq, wkv, main, fifth, dim)

    def slab(lo, hi):
        return jnp.where(co == co0, held[lo * chunk : hi * chunk], from_core[lo * chunk : hi * chunk])

    rel = (y - y0) % NY
    up = send(slab(2, 5), y_step(1))
    down = send(slab(5, 8), y_step(-1))

    width = depth // NX
    pair_0 = send(lax.dynamic_slice(mine, (0, x * width), (rows, width)), z_pair)
    other_lens = [send(lengths, to)[0] for to in (z_pair, other_core, z_pair_other_core)]
    up, down, pair_0, *other_lens = lax.optimization_barrier((up, down, pair_0, *other_lens))
    pair_up, pair_down = send(pair_0, x_step(1)), send(pair_0, x_step(-1))
    pair_far = [send(pair_up[: rows // 2], x_step(1)), send(pair_down[rows // 2 :], x_step(-1))]

    far = send(up[2 * chunk :], y_step(1)), send(down[:chunk], y_step(-1))
    got = [
        jnp.where(
            rel == 0,
            slab(p, p + 1),
            jnp.where(
                rel == 1,
                up[p * chunk : (p + 1) * chunk],
                jnp.where(rel == 2, far[p], down[(p + 1) * chunk : (p + 2) * chunk]),
            ),
        )
        for p in range(2)
    ]
    odd = z % 2
    mirrored = send(jnp.where(odd == 0, got[1], got[0]), z_mirror)
    own = jnp.where(zh == zh0, jnp.where(odd == 0, got[0], got[1]), mirrored)

    zs = (z + jnp.array([0, NZ - 2, 2, 4])) % NZ
    quarter = jnp.where(zs // NZL == zh0, zs % NZL, NZL - 1 - zs % NZL)
    rels = (rel + jnp.array([0, NY - 1, 1, 2])) % NY
    place = (quarter[:, None] * NY + rels[None, :]).reshape(-1).astype(jnp.int32)
    turn = (quarter - x) % NX
    slot = jnp.where(turn == 0, 0, jnp.where(turn == 3, 1, jnp.where(turn == 1, 2, 3)))
    slot = jnp.repeat(slot, NY).astype(jnp.int32)

    n0 = own
    own, pair_0, pair_up, pair_down, *pair_far = lax.optimization_barrier((own, pair_0, pair_up, pair_down, *pair_far))
    z_up, z_down = send(own, z_step(2)), send(own, z_step(-2))
    y_up0, y_down0 = send(own, y_step(1)), send(own, y_step(-1))
    here = order_tokens(place, slot, main, mine, [pair_0, pair_up, pair_down] + pair_far)
    z_up, z_down, y_up0, y_down0, *here = lax.optimization_barrier((z_up, z_down, y_up0, y_down0, *here))
    n1 = jnp.concatenate([z_up, z_down], 0)
    y_up1, y_down1 = send(n1, y_step(1)), send(n1, y_step(-1))
    z_far = [send(z_up[:cut], z_step(2)), send(z_down[cut:], z_step(-2))]
    there = [send(here[0], other_core)]
    y_far0 = [send(y_up0[:cut], y_step(1)), send(y_down0[cut:], y_step(-1))]
    y_up1, y_down1, z_far[0], z_far[1], y_far0[0], y_far0[1], there[0] = lax.optimization_barrier(
        (y_up1, y_down1, *z_far, *y_far0, *there)
    )
    n2 = jnp.concatenate(z_far, 0)
    y_up2, y_down2 = send(n2, y_step(1)), send(n2, y_step(-1))
    y_far1 = [send(y_up1[:chunk], y_step(1)), send(y_down1[chunk:], y_step(-1))]
    all_lens = jnp.concatenate([lens] + other_lens)
    cosine, sine = rope_tables(all_lens.astype(jnp.float32), dim)

    def whole(c):
        return [(c, 0, chunk)]

    top, bottom = (0, cut), (cut, chunk - cut)
    acc = project(
        co,
        here[0],
        there[0],
        [n0, y_up0, y_down0] + y_far0 + [n1, y_up1, y_down1],
        [whole(0), whole(1), whole(2), [(3,) + top], [(3,) + bottom]]
        + [whole(NY + i) + whole(2 * NY + i) for i in range(3)],
        main,
        None,
        None,
    )
    y_up2, y_down2, y_far1[0], y_far1[1], acc, here[1] = lax.optimization_barrier(
        (y_up2, y_down2, *y_far1, acc, here[1])
    )
    there.append(send(here[1], other_core))
    y_far2 = [send(y_up2[:cut], y_step(1)), send(y_down2[cut:], y_step(-1))]
    out = project(
        co,
        here[1],
        there[1],
        y_far1 + [n2, y_up2, y_down2] + y_far2,
        [whole(NY + 3), whole(2 * NY + 3)]
        + [whole(3 * NY + i) for i in range(3)]
        + [[(3 * NY + 3,) + top], [(3 * NY + 3,) + bottom]],
        main,
        acc,
        (cosine, sine),
    )
    near = [out[:rows], send(out[2 * rows : 3 * rows], other_core)]
    far = [
        send(out[rows : 2 * rows, : 3 * dim], z_pair),
        send(out[3 * rows :, : 3 * dim], z_pair_other_core),
    ]
    columns = jnp.stack(
        [4 * odd + 2 * co, 4 * odd + 2 * (1 - co), 4 * (1 - odd) + 2 * co, 4 * (1 - odd) + 2 * (1 - co)]
    ).astype(jnp.int32)

    index = jnp.arange(rows)
    before = (lens[None, :] < lens[:, None]) | ((lens[None, :] == lens[:, None]) & (index[None, :] < index[:, None]))
    rank = jnp.sum(before.astype(jnp.int32), 1)
    hot = rank[None, :] == index[:, None]
    sorted_lens = jnp.sum(jnp.where(hot, lens[None, :], 0), 1)
    perm, back = hot.astype(jnp.bfloat16), hot.T.astype(jnp.bfloat16)
    context = cache_keys.shape[1]
    block, key_block = math.gcd(rows, 64), math.gcd(context, 1024)
    groups = sorted_lens.reshape(rows // block, block)
    bounds = ((groups[:, -1] + key_block - 1) // key_block).astype(jnp.int32)
    lens_wide = jnp.broadcast_to(sorted_lens[:, None], (rows, dim))
    keys_t, values = cache_keys[0].T, resident_value_cache[0]
    four = (4, rows, dim)
    scores = pltpu.VMEM((2, 4 * block, context), jnp.float32)
    early = attention_call(
        functools.partial(early_kernel, block, key_block),
        [jax.ShapeDtypeStruct(four, jnp.bfloat16)] + [jax.ShapeDtypeStruct(four, jnp.float32)] * 3,
        [scores],
        1,
        (bounds, *near, perm, lens_wide, keys_t, values),
        rows, context, dim,
    )
    result = attention_call(
        functools.partial(late_kernel, block, key_block),
        jax.ShapeDtypeStruct((rows, 8 * dim), jnp.bfloat16),
        [
            pltpu.VMEM(four, jnp.bfloat16),
            scores,
            pltpu.VMEM((2, rows, dim), jnp.float32),
            pltpu.VMEM((8, rows, dim), jnp.bfloat16),
        ],
        3,
        (odd.reshape(1).astype(jnp.int32), columns, bounds, *near, *far, *early)
        + (cosine[:rows], sine[:rows], perm, back, lens_wide, keys_t, values),
        rows, context, dim,
    )
    return result[None]


def solution(mesh):
    fine = Mesh(mesh.devices.reshape(NY, NZH, NCO, NX, NZL), AXES)
    layer = ("y", "z_hi", "core")
    return jax.shard_map(
        local,
        mesh=fine,
        in_specs=(
            P("dp", layer, None),
            P("dp", layer),
            P(),
            P(layer, "dp", "head"),
            P(layer, "dp", "head", None),
            P("dp", None, "head"),
            P("dp", None, "head"),
        ),
        out_specs=P("dp", layer, "head"),
        check_vma=False,
    )
```

```python
import functools
import math

import jax
import jax.numpy as jnp
from jax import lax
from jax.experimental import pallas as pl
from jax.experimental.pallas import tpu as pltpu
from jax.sharding import Mesh, PartitionSpec as P

rope_base = 500000.0
AXES = ("y", "z_hi", "core", "head", "dp")
NY, NZH, NCO, NX, NZL = 4, 2, 2, 4, 4
NZ = NZH * NZL
VMEM = pl.BlockSpec(memory_space=pltpu.VMEM)
SMEM = pl.BlockSpec(memory_space=pltpu.SMEM)
ANY = pl.BlockSpec(memory_space=pl.ANY)
EARLY_CHUNKS = (0, 1, 2, 4, 5, 6, 8, 9, 10)
LATE_CHUNKS = (3, 7, 11, 12, 13, 14, 15)


def linear(y, z, co, x):
    y, z, x = y % NY, z % NZ, x % NX
    return (((y * NZH + z // NZL) * NCO + co) * NX + x) * NZL + z % NZL


def moves(to):
    pairs = []
    for y in range(NY):
        for z in range(NZ):
            for co in range(NCO):
                for x in range(NX):
                    pairs.append((linear(y, z, co, x), linear(*to(y, z, co, x))))
    return pairs


def send(block, to):
    return lax.ppermute(block, AXES, moves(to))


def y_step(n):
    return lambda y, z, co, x: (y + n, z, co, x)


def z_step(n):
    return lambda y, z, co, x: (y, z + n, co, x)


def x_step(n):
    return lambda y, z, co, x: (y, z, co, x + n)


def other_core(y, z, co, x):
    return (y, z, 1 - co, x)


def z_pair(y, z, co, x):
    return (y, z ^ 1, co, x)


def z_pair_other_core(y, z, co, x):
    return (y, z ^ 1, 1 - co, x)


def z_mirror(y, z, co, x):
    return (y, NZ - 1 - z, co, x)


def after(block, *others):
    return lax.optimization_barrier((block,) + others)[0]


def run_all(copies):
    for copy in copies:
        copy.start()
    for copy in copies:
        copy.wait()


def pack_kernel(main, fifth, dim, core_ref, wq_ref, wkv_ref, out_ref, sems):
    core = core_ref[0]
    copies = []
    for piece in range(NY):
        for half in range(2):
            base = (piece * 2 + half) * (main + fifth)
            first_row = piece * main
            column = pl.multiple_of(half * 4 * dim + core * 2 * dim, dim)
            copies.append((wq_ref.at[first_row : first_row + main, pl.ds(column, 2 * dim)], out_ref.at[base : base + main, :]))
            for side in range(2):
                row = pl.multiple_of(first_row + core * 2 * fifth + side * fifth, fifth)
                copies.append(
                    (
                        wkv_ref.at[pl.ds(row, fifth), half * dim : (half + 1) * dim],
                        out_ref.at[base + main : base + main + fifth, side * dim : (side + 1) * dim],
                    )
                )
    run_all([pltpu.make_async_copy(src, dst, sems.at[i]) for i, (src, dst) in enumerate(copies)])


def pack(core, wq, wkv, main, fifth, dim):
    return pl.pallas_call(
        functools.partial(pack_kernel, main, fifth, dim),
        out_shape=jax.ShapeDtypeStruct((NY * 2 * (main + fifth), 2 * dim), wq.dtype),
        in_specs=[SMEM, ANY, ANY],
        out_specs=VMEM,
        scratch_shapes=[pltpu.SemaphoreType.DMA((NY * 6,))],
        compiler_params=pltpu.CompilerParams(vmem_limit_bytes=60 * 2**20),
        cost_estimate=pl.CostEstimate(flops=0, bytes_accessed=5 * 2**20, transcendentals=0),
    )(core.reshape(1), wq, wkv)


def order_kernel(wide, place_ref, slot_ref, mine_ref, same_ref, up_ref, down_ref, far_up_ref, far_down_ref, early_ref, late_ref, sems):
    rows = mine_ref.shape[0]
    per_quarter = same_ref.shape[1] // wide
    half = rows // 2
    held = [(same_ref, 0, 0, rows), (up_ref, 1, 0, rows), (down_ref, 2, 0, rows)]
    held += [(far_up_ref, 3, 0, half), (far_down_ref, 3, half, half)]
    at = 0
    for out_ref, chunks in ((early_ref, EARLY_CHUNKS), (late_ref, LATE_CHUNKS)):
        for i, chunk in enumerate(chunks):
            place = place_ref[chunk]
            column = pl.multiple_of(place * wide, wide)
            pltpu.make_async_copy(mine_ref.at[:, pl.ds(column, wide)], out_ref.at[i, :rows, :], sems.at[at]).start()
            at += 1
            inner = pl.multiple_of(place % per_quarter * wide, wide)
            for ref, slot, first, n in held:

                @pl.when(slot_ref[chunk] == slot)
                def _(ref=ref, first=first, n=n, inner=inner, out_ref=out_ref, i=i, sem=at + (first > 0)):
                    pltpu.make_async_copy(
                        ref.at[:, pl.ds(inner, wide)], out_ref.at[i, rows + first : rows + first + n, :], sems.at[sem]
                    ).start()

            at += 2
    at = 0
    for out_ref, chunks in ((early_ref, EARLY_CHUNKS), (late_ref, LATE_CHUNKS)):
        for i, chunk in enumerate(chunks):
            block = out_ref.at[i, :rows, :]
            pltpu.make_async_copy(block, block, sems.at[at]).wait()
            for ref, slot, first, n in held:

                @pl.when(slot_ref[chunk] == slot)
                def _(first=first, n=n, out_ref=out_ref, i=i, sem=at + 1 + (first > 0)):
                    block = out_ref.at[i, rows + first : rows + first + n, :]
                    pltpu.make_async_copy(block, block, sems.at[sem]).wait()

            at += 3


def order_tokens(place, slot, wide, mine, pieces):
    rows, depth = mine.shape
    return pl.pallas_call(
        functools.partial(order_kernel, wide),
        out_shape=[
            jax.ShapeDtypeStruct((len(chunks), 2 * rows, wide), mine.dtype) for chunks in (EARLY_CHUNKS, LATE_CHUNKS)
        ],
        in_specs=[SMEM, SMEM] + [ANY] * 6,
        out_specs=[VMEM, VMEM],
        scratch_shapes=[pltpu.SemaphoreType.DMA((3 * NY * NZL,))],
        compiler_params=pltpu.CompilerParams(vmem_limit_bytes=20 * 2**20),
        cost_estimate=pl.CostEstimate(flops=0, bytes_accessed=8 * rows * depth, transcendentals=0),
    )(place, slot, mine, *pieces)


def project_kernel(parts, main, chunks, first, last, core_ref, tokens_ref, others_ref, *rest):
    rest = list(rest)
    start_ref = None if first else rest.pop(0)
    cos_ref, sin_ref = (rest.pop(0), rest.pop(0)) if last else (None, None)
    weights, out_ref = rest[: len(parts)], rest[len(parts)]
    acc = rest[len(parts) + 1] if last else out_ref
    two = weights[0].shape[1]
    dim = two // 2
    core = core_ref[0]
    rows = tokens_ref.shape[1]
    acc[...] = jnp.zeros_like(acc) if first else start_ref[...]
    column = pl.multiple_of(core * (main // 2), main // 2)
    for w_ref, part in zip(weights, parts):
        at = 0
        for chunk, begin, n in part:
            i = chunks.index(chunk)
            end = min(begin + n, main)
            for side, ref in enumerate((tokens_ref, others_ref)):
                cut = slice(side * rows, (side + 1) * rows)
                acc[cut, :two] += jnp.dot(
                    ref[i, :, begin:end], w_ref[at : at + end - begin, :], preferred_element_type=jnp.float32
                )
                if begin + n > main:
                    low = at + main - begin
                    packed = w_ref[low : low + main // 4, :]
                    w = jnp.concatenate([packed[:, :dim], packed[:, dim:]], 0)
                    acc[cut, two:] += jnp.dot(
                        ref[i, :, pl.ds(column, main // 2)], w, preferred_element_type=jnp.float32
                    )
            at += n
    if last:
        for h in range(2):
            x = acc[:, h * dim : (h + 1) * dim]
            out = x * cos_ref[...] + pltpu.roll(x, dim // 2, 1) * sin_ref[...]
            out_ref[:, h * dim : (h + 1) * dim] = out.astype(jnp.bfloat16)
        x = acc[:, two:]
        high = x.astype(jnp.bfloat16)
        out_ref[:, two : two + dim] = high
        out_ref[:, two + dim :] = (x - high.astype(jnp.float32)).astype(jnp.bfloat16)


def project(core, tokens, others, weights, parts, main, chunks, start, tables):
    rows = 2 * tokens.shape[1]
    cols = weights[0].shape[1]
    first, last = start is None, tables is not None
    extra = ([] if first else [start]) + (list(tables) if last else [])
    taken = sum(w.shape[0] for w in weights)
    acc_shape = (rows, cols + cols // 2)
    return pl.pallas_call(
        functools.partial(project_kernel, parts, main, chunks, first, last),
        out_shape=jax.ShapeDtypeStruct((rows, 2 * cols), jnp.bfloat16)
        if last
        else jax.ShapeDtypeStruct(acc_shape, jnp.float32),
        in_specs=[SMEM] + [VMEM] * (2 + len(extra) + len(weights)),
        out_specs=VMEM,
        scratch_shapes=[pltpu.VMEM(acc_shape, jnp.float32)] if last else [],
        compiler_params=pltpu.CompilerParams(vmem_limit_bytes=22 * 2**20),
        cost_estimate=pl.CostEstimate(
            flops=2 * rows * taken * cols, bytes_accessed=2 * taken * (rows + cols), transcendentals=0
        ),
    )(core, tokens, others, *extra, *weights)


def rope_tables(places, head_dim):
    channel = jnp.arange(head_dim // 2).astype(jnp.float32)
    rates = jnp.power(jnp.float32(rope_base), -2.0 * channel / head_dim)
    angles = places[:, None] * rates
    cosine, sine = jnp.cos(angles), jnp.sin(angles)
    return jnp.concatenate([cosine, cosine], -1), jnp.concatenate([-sine, sine], -1)


def sort_rows(perm_ref, x):
    return jnp.dot(perm_ref[...], x, preferred_element_type=jnp.float32).astype(jnp.bfloat16)


def over_cache(block, key_block, bounds_ref, lens_ref, kt_ref, v_ref, qs, scores, put):
    heads, rows, dim = qs.shape
    m_rows = heads * block
    scale = jnp.float32(math.log2(math.e) / math.sqrt(dim))
    tiles = key_block // dim
    count = rows // block

    def score(b, j, peak):
        off = pl.multiple_of(j * key_block, key_block)
        q = qs[:, b * block : (b + 1) * block, :].reshape(m_rows, dim)
        left = lens_ref[b * block : (b + 1) * block, :] - off
        lane = lax.broadcasted_iota(jnp.int32, (block, dim), 1)
        s = jnp.dot(q, kt_ref[:, pl.ds(off, key_block)], preferred_element_type=jnp.float32)
        for t in range(tiles):
            seen = lane < left - t * dim
            tile = jnp.concatenate(
                [
                    jnp.where(seen, s[h * block : (h + 1) * block, t * dim : (t + 1) * dim], -1e30)
                    for h in range(heads)
                ],
                0,
            )
            scores[b % 2, :, pl.ds(off + t * dim, dim)] = tile
            peak = jnp.maximum(peak, tile)
        return peak

    def mix(b, j, shift, sums):
        total, mixed = sums
        off = pl.multiple_of(j * key_block, key_block)
        low_bits = []
        for t in range(tiles):
            w = jnp.exp2(scores[b % 2, :, pl.ds(off + t * dim, dim)] * scale - shift)
            total = total + w
            low_bits.append(w.astype(jnp.bfloat16))
        mixed = mixed + jnp.dot(
            jnp.concatenate(low_bits, 1), v_ref[pl.ds(off, key_block), :], preferred_element_type=jnp.float32
        )
        return total, mixed

    zero = jnp.zeros((m_rows, dim), jnp.float32)
    lowest = jnp.full((m_rows, dim), -1e30, jnp.float32)
    peak, shift, before = None, None, 0
    for b in range(count + 1):
        now = bounds_ref[b] if b < count else 0
        peak_next, sums = lowest, (zero, zero)
        if b == 0:
            peak_next = lax.fori_loop(0, now, lambda j, p: score(0, j, p), peak_next)
        elif b < count:

            def step(j, carry, b=b, shift=shift):
                return score(b, j, carry[0]), mix(b - 1, j, shift, carry[1])

            peak_next, sums = lax.fori_loop(0, before, step, (peak_next, sums))
            peak_next = lax.fori_loop(before, now, lambda j, p, b=b: score(b, j, p), peak_next)
        else:
            sums = lax.fori_loop(0, before, lambda j, s, b=b, shift=shift: mix(b - 1, j, shift, s), sums)
        if b > 0:
            total = jnp.broadcast_to(jnp.sum(sums[0], -1, keepdims=True), (m_rows, dim))
            put((b - 1) * block, peak, total, sums[1])
        if b < count:
            peak = jnp.broadcast_to(jnp.max(peak_next, -1, keepdims=True), (m_rows, dim))
            shift = peak * scale
        before = now


def keep(refs, heads, block):
    def put(r0, *values):
        for ref, value in zip(refs, values):
            ref[:, r0 : r0 + block, :] = value.reshape(heads, block, value.shape[1])

    return put


def early_kernel(block, key_block, bounds_ref, a_ref, b_ref, perm_ref, lens_ref, kt_ref, v_ref, *rest):
    outs, scores = rest[:4], rest[4]
    qs = outs[0]
    dim = qs.shape[2]
    for i, ref in enumerate((a_ref, b_ref)):
        for h in range(2):
            qs[2 * i + h] = sort_rows(perm_ref, ref[:, h * dim : (h + 1) * dim])
    put = keep(outs[1:], 4, block)
    over_cache(block, key_block, bounds_ref, lens_ref, kt_ref, v_ref, qs, scores, put)


def late_kernel(block, key_block, half_ref, column_ref, bounds_ref, *rest):
    parts, early, rest = rest[:4], rest[4:8], rest[8:]
    cos_ref, sin_ref, perm_ref, back_ref, lens_ref, kt_ref, v_ref, out_ref, qs, scores, fresh, result = rest
    dim = qs.shape[2]
    scale = jnp.float32(math.log2(math.e) / math.sqrt(dim))
    for i, ref in enumerate(parts[2:]):
        for h in range(2):
            qs[2 * i + h] = sort_rows(perm_ref, ref[:, h * dim : (h + 1) * dim])
    sums = [
        sum(ref[:, c : c + dim].astype(jnp.float32) for c in range(2 * dim, ref.shape[1], dim)) for ref in parts
    ]
    near, far = sums[0] + sums[1], sums[2] + sums[3]
    first = half_ref[0] == 0
    key = jnp.where(first, near, far)
    key = key * cos_ref[...] + pltpu.roll(key, dim // 2, 1) * sin_ref[...]
    fresh[0] = sort_rows(perm_ref, key.astype(jnp.bfloat16)).astype(jnp.float32)
    fresh[1] = sort_rows(perm_ref, jnp.where(first, far, near).astype(jnp.bfloat16)).astype(jnp.float32)

    def finish(q, cut, peak, total, mixed):
        own = jnp.sum(q.astype(jnp.float32) * fresh[0, cut, :], -1, keepdims=True)
        top = jnp.maximum(peak, own)
        shrink = jnp.exp2((peak - top) * scale)
        own_weight = jnp.exp2((own - top) * scale)
        low = own_weight.astype(jnp.bfloat16).astype(jnp.float32)
        value = mixed * shrink + low * fresh[1, cut, :]
        return (value / (total * shrink + own_weight)).astype(jnp.bfloat16)

    def put(r0, peak, total, mixed):
        cut = slice(r0, r0 + block)
        for h in range(4):
            at = slice(h * block, (h + 1) * block)
            result[4 + h, cut, :] = finish(qs[h, cut, :], cut, peak[at], total[at], mixed[at])
            result[h, cut, :] = finish(*[early[0][h, cut, :], cut] + [ref[h, cut, :] for ref in early[1:]])

    over_cache(block, key_block, bounds_ref, lens_ref, kt_ref, v_ref, qs, scores, put)
    for i in range(4):
        for h in range(2):
            column = pl.multiple_of((column_ref[i] + h) * dim, dim)
            rows_back = jnp.dot(back_ref[...], result[2 * i + h], preferred_element_type=jnp.float32)
            out_ref[:, pl.ds(column, dim)] = rows_back.astype(jnp.bfloat16)


def attention_call(kernel, out_shape, scratch, smem, args, rows, context, dim):
    heads = 4
    many = isinstance(out_shape, list)
    return pl.pallas_call(
        kernel,
        out_shape=out_shape,
        in_specs=[SMEM] * smem + [VMEM] * (len(args) - smem),
        out_specs=[VMEM] * len(out_shape) if many else VMEM,
        scratch_shapes=scratch,
        compiler_params=pltpu.CompilerParams(vmem_limit_bytes=30 * 2**20),
        cost_estimate=pl.CostEstimate(
            flops=4 * heads * rows * context * dim,
            bytes_accessed=4 * context * dim,
            transcendentals=heads * rows * context,
        ),
    )(*args)


def local(tokens, lengths, owner, wq_slabs, wkv_slabs, cache_keys, resident_value_cache):
    mine = tokens[0]
    lens = lengths[0]
    rows, depth = mine.shape
    dim = cache_keys.shape[2]
    part = wq_slabs.shape[1]
    y, zh, co, x, zl = (lax.axis_index(name) for name in AXES)
    z = zh * NZL + zl
    holder = owner[0] % (NY * NZH * NCO)
    y0, zh0, co0 = holder // (NZH * NCO), holder // NCO % NZH, holder % NCO
    main = part // NY
    fifth = main // 4
    chunk = main + fifth
    cut = main * 3 // 4

    wq, wkv = wq_slabs[0], wkv_slabs[0, :, 0]
    from_core = send(pack(1 - co, wq, wkv, main, fifth, dim), other_core)
    held = pack(co, wq, wkv, main, fifth, dim)

    def slab(lo, hi):
        return jnp.where(co == co0, held[lo * chunk : hi * chunk], from_core[lo * chunk : hi * chunk])

    rel = (y - y0) % NY
    up = send(slab(2, 5), y_step(1))
    down = send(slab(5, 8), y_step(-1))

    width = depth // NX
    pair_0 = send(lax.dynamic_slice(mine, (0, x * width), (rows, width)), z_pair)
    other_lens = [send(lengths, to)[0] for to in (z_pair, other_core, z_pair_other_core)]
    pair_up, pair_down = send(pair_0, x_step(1)), send(pair_0, x_step(-1))
    pair_far = [send(pair_up[: rows // 2], x_step(1)), send(pair_down[rows // 2 :], x_step(-1))]

    zs = (z + jnp.array([0, NZ - 2, 2, 4])) % NZ
    quarter = jnp.where(zs // NZL == zh0, zs % NZL, NZL - 1 - zs % NZL)
    rels = (rel + jnp.array([0, NY - 1, 1, 2])) % NY
    place = (quarter[:, None] * NY + rels[None, :]).reshape(-1).astype(jnp.int32)
    turn = (quarter - x) % NX
    slot = jnp.where(turn == 0, 0, jnp.where(turn == 3, 1, jnp.where(turn == 1, 2, 3)))
    slot = jnp.repeat(slot, NY).astype(jnp.int32)

    index = jnp.arange(rows)
    before = (lens[None, :] < lens[:, None]) | ((lens[None, :] == lens[:, None]) & (index[None, :] < index[:, None]))
    rank = jnp.sum(before.astype(jnp.int32), 1)
    hot = rank[None, :] == index[:, None]
    sorted_lens = jnp.sum(jnp.where(hot, lens[None, :], 0), 1)
    perm, back = hot.astype(jnp.bfloat16), hot.T.astype(jnp.bfloat16)
    context = cache_keys.shape[1]
    block, key_block = math.gcd(rows, 64), math.gcd(context, 1024)
    groups = sorted_lens.reshape(rows // block, block)
    bounds = ((groups[:, -1] + key_block - 1) // key_block).astype(jnp.int32)
    lens_wide = jnp.broadcast_to(sorted_lens[:, None], (rows, dim))
    keys_t, values = cache_keys[0].T, resident_value_cache[0]
    odd = z % 2
    columns = jnp.stack(
        [4 * odd + 2 * co, 4 * odd + 2 * (1 - co), 4 * (1 - odd) + 2 * co, 4 * (1 - odd) + 2 * (1 - co)]
    ).astype(jnp.int32)
    cores, odds = co.reshape(1), odd.reshape(1).astype(jnp.int32)
    up, down, place, slot, perm, back, lens_wide, keys_t, bounds, columns, cores, odds = lax.optimization_barrier(
        (up, down, place, slot, perm, back, lens_wide, keys_t, bounds, columns, cores, odds)
    )

    far = send(up[2 * chunk :], y_step(1)), send(down[:chunk], y_step(-1))
    got = [
        jnp.where(
            rel == 0,
            slab(p, p + 1),
            jnp.where(
                rel == 1,
                up[p * chunk : (p + 1) * chunk],
                jnp.where(rel == 2, far[p], down[(p + 1) * chunk : (p + 2) * chunk]),
            ),
        )
        for p in range(2)
    ]
    mirrored = send(jnp.where(odd == 0, got[1], got[0]), z_mirror)
    own = jnp.where(zh == zh0, jnp.where(odd == 0, got[0], got[1]), mirrored)

    n0 = own
    own, pair_0, pair_up, pair_down, pair_far[0], pair_far[1], *other_lens = lax.optimization_barrier(
        (own, pair_0, pair_up, pair_down, *pair_far, *other_lens)
    )
    z_up, z_down = send(own, z_step(2)), send(own, z_step(-2))
    y_up0, y_down0 = send(own, y_step(1)), send(own, y_step(-1))
    here = order_tokens(place, slot, main, mine, [pair_0, pair_up, pair_down] + pair_far)
    z_up, z_down, y_up0, y_down0, *here = lax.optimization_barrier((z_up, z_down, y_up0, y_down0, *here))
    n1 = jnp.concatenate([z_up, z_down], 0)
    y_up1, y_down1 = send(n1, y_step(1)), send(n1, y_step(-1))
    n2 = send(z_up, z_step(2))
    there = [send(here[0], other_core)]

    all_lens = jnp.concatenate([lens] + other_lens)
    cosine, sine = rope_tables(all_lens.astype(jnp.float32), dim)

    y_up1, y_down1, n2, there[0], cosine, sine = lax.optimization_barrier(
        (y_up1, y_down1, n2, *there, cosine, sine)
    )
    y_up2, y_down2 = send(n2, y_step(1)), send(n2, y_step(-1))
    y_far1 = [
        send(jnp.concatenate([y_up0[:cut], y_up1[:chunk]], 0), y_step(1)),
        send(jnp.concatenate([y_down0[cut:], y_down1[chunk:]], 0), y_step(-1)),
    ]
    def whole(c):
        return [(c, 0, chunk)]

    top, bottom = (0, cut), (cut, chunk - cut)
    acc = project(
        cores,
        here[0],
        there[0],
        [n0, y_up0, y_down0, n1, y_up1, y_down1],
        [whole(0), whole(1), whole(2)] + [whole(NY + i) + whole(2 * NY + i) for i in range(3)],
        main,
        EARLY_CHUNKS,
        None,
        None,
    )
    y_up2, y_down2, y_far1[0], y_far1[1], acc, here[1] = lax.optimization_barrier(
        (y_up2, y_down2, *y_far1, acc, here[1])
    )
    there.append(send(here[1], other_core))
    y_far2 = [send(y_up2[:cut], y_step(1)), send(y_down2[cut:], y_step(-1))]
    acc = project(
        cores,
        here[1],
        there[1],
        y_far1 + [n2, y_up2, y_down2],
        [[(3,) + top] + whole(NY + 3), [(3,) + bottom] + whole(2 * NY + 3)] + [whole(3 * NY + i) for i in range(3)],
        main,
        LATE_CHUNKS,
        acc,
        None,
    )
    out = project(
        cores,
        here[1][-1:],
        there[1][-1:],
        y_far2,
        [[(3 * NY + 3,) + top], [(3 * NY + 3,) + bottom]],
        main,
        LATE_CHUNKS[-1:],
        acc,
        (cosine, sine),
    )
    near = [out[:rows], send(out[2 * rows : 3 * rows], other_core)]
    far = [
        send(out[rows : 2 * rows, : 3 * dim], z_pair),
        send(out[3 * rows :, : 3 * dim], z_pair_other_core),
    ]

    four = (4, rows, dim)
    scores = pltpu.VMEM((2, 4 * block, context), jnp.float32)
    early = attention_call(
        functools.partial(early_kernel, block, key_block),
        [jax.ShapeDtypeStruct(four, jnp.bfloat16)] + [jax.ShapeDtypeStruct(four, jnp.float32)] * 3,
        [scores],
        1,
        (bounds, *near, perm, lens_wide, keys_t, values),
        rows, context, dim,
    )
    result = attention_call(
        functools.partial(late_kernel, block, key_block),
        jax.ShapeDtypeStruct((rows, 8 * dim), jnp.bfloat16),
        [
            pltpu.VMEM(four, jnp.bfloat16),
            scores,
            pltpu.VMEM((2, rows, dim), jnp.float32),
            pltpu.VMEM((8, rows, dim), jnp.bfloat16),
        ],
        3,
        (odds, columns, bounds, *near, *far, *early)
        + (cosine[:rows], sine[:rows], perm, back, lens_wide, keys_t, values),
        rows, context, dim,
    )
    return result[None]


def solution(mesh):
    fine = Mesh(mesh.devices.reshape(NY, NZH, NCO, NX, NZL), AXES)
    layer = ("y", "z_hi", "core")
    return jax.shard_map(
        local,
        mesh=fine,
        in_specs=(
            P("dp", layer, None),
            P("dp", layer),
            P(),
            P(layer, "dp", "head"),
            P(layer, "dp", "head", None),
            P("dp", None, "head"),
            P("dp", None, "head"),
        ),
        out_specs=P("dp", layer, "head"),
        check_vma=False,
    )
```

```python
import functools
import math

import jax
import jax.numpy as jnp
from jax import lax
from jax.experimental import pallas as pl
from jax.experimental.pallas import tpu as pltpu
from jax.sharding import Mesh, PartitionSpec as P

rope_base = 500000.0
AXES = ("y", "z_hi", "core", "head", "dp")
NY, NZH, NCO, NX, NZL = 4, 2, 2, 4, 4
NZ = NZH * NZL
VMEM = pl.BlockSpec(memory_space=pltpu.VMEM)
SMEM = pl.BlockSpec(memory_space=pltpu.SMEM)
ANY = pl.BlockSpec(memory_space=pl.ANY)
EARLY_CHUNKS = (0, 1, 2, 4, 5, 6, 8, 9, 10)
LATE_CHUNKS = (3, 7, 11, 12, 13, 14, 15)
CHUNKS = EARLY_CHUNKS + LATE_CHUNKS


def linear(y, z, co, x):
    y, z, x = y % NY, z % NZ, x % NX
    return (((y * NZH + z // NZL) * NCO + co) * NX + x) * NZL + z % NZL


def moves(to):
    pairs = []
    for y in range(NY):
        for z in range(NZ):
            for co in range(NCO):
                for x in range(NX):
                    pairs.append((linear(y, z, co, x), linear(*to(y, z, co, x))))
    return pairs


def send(block, to):
    return lax.ppermute(block, AXES, moves(to))


def y_step(n):
    return lambda y, z, co, x: (y + n, z, co, x)


def z_step(n):
    return lambda y, z, co, x: (y, z + n, co, x)


def x_step(n):
    return lambda y, z, co, x: (y, z, co, x + n)


def other_core(y, z, co, x):
    return (y, z, 1 - co, x)


def z_pair(y, z, co, x):
    return (y, z ^ 1, co, x)


def z_pair_other_core(y, z, co, x):
    return (y, z ^ 1, 1 - co, x)


def z_mirror(y, z, co, x):
    return (y, NZ - 1 - z, co, x)


def after(block, *others):
    return lax.optimization_barrier((block,) + others)[0]


def run_all(copies):
    for copy in copies:
        copy.start()
    for copy in copies:
        copy.wait()


def pack_kernel(main, fifth, dim, core_ref, wq_ref, wkv_ref, out_ref, sems):
    core = core_ref[0]
    copies = []
    for piece in range(NY):
        for half in range(2):
            base = (piece * 2 + half) * (main + fifth)
            first_row = piece * main
            column = pl.multiple_of(half * 4 * dim + core * 2 * dim, dim)
            copies.append((wq_ref.at[first_row : first_row + main, pl.ds(column, 2 * dim)], out_ref.at[base : base + main, :]))
            for side in range(2):
                row = pl.multiple_of(first_row + core * 2 * fifth + side * fifth, fifth)
                copies.append(
                    (
                        wkv_ref.at[pl.ds(row, fifth), half * dim : (half + 1) * dim],
                        out_ref.at[base + main : base + main + fifth, side * dim : (side + 1) * dim],
                    )
                )
    run_all([pltpu.make_async_copy(src, dst, sems.at[i]) for i, (src, dst) in enumerate(copies)])


def pack(core, wq, wkv, main, fifth, dim):
    return pl.pallas_call(
        functools.partial(pack_kernel, main, fifth, dim),
        out_shape=jax.ShapeDtypeStruct((NY * 2 * (main + fifth), 2 * dim), wq.dtype),
        in_specs=[SMEM, ANY, ANY],
        out_specs=VMEM,
        scratch_shapes=[pltpu.SemaphoreType.DMA((NY * 6,))],
        compiler_params=pltpu.CompilerParams(vmem_limit_bytes=60 * 2**20),
        cost_estimate=pl.CostEstimate(flops=0, bytes_accessed=5 * 2**20, transcendentals=0),
    )(core.reshape(1), wq, wkv)


def order_kernel(wide, place_ref, slot_ref, mine_ref, same_ref, up_ref, down_ref, far_up_ref, far_down_ref, out_ref, sems):
    rows = mine_ref.shape[0]
    per_quarter = same_ref.shape[1] // wide
    half = rows // 2
    held = [(same_ref, 0, 0, rows), (up_ref, 1, 0, rows), (down_ref, 2, 0, rows)]
    held += [(far_up_ref, 3, 0, half), (far_down_ref, 3, half, half)]
    for i, chunk in enumerate(CHUNKS):
        place = place_ref[chunk]
        column = pl.multiple_of(place * wide, wide)
        pltpu.make_async_copy(mine_ref.at[:, pl.ds(column, wide)], out_ref.at[i, :rows, :], sems.at[3 * i]).start()
        inner = pl.multiple_of(place % per_quarter * wide, wide)
        for ref, slot, first, n in held:

            @pl.when(slot_ref[chunk] == slot)
            def _(ref=ref, first=first, n=n, inner=inner, i=i):
                pltpu.make_async_copy(
                    ref.at[:, pl.ds(inner, wide)],
                    out_ref.at[i, rows + first : rows + first + n, :],
                    sems.at[3 * i + 1 + (first > 0)],
                ).start()

    for i, chunk in enumerate(CHUNKS):
        block = out_ref.at[i, :rows, :]
        pltpu.make_async_copy(block, block, sems.at[3 * i]).wait()
        for ref, slot, first, n in held:

            @pl.when(slot_ref[chunk] == slot)
            def _(first=first, n=n, i=i):
                block = out_ref.at[i, rows + first : rows + first + n, :]
                pltpu.make_async_copy(block, block, sems.at[3 * i + 1 + (first > 0)]).wait()


def order_tokens(place, slot, wide, mine, pieces):
    rows, depth = mine.shape
    return pl.pallas_call(
        functools.partial(order_kernel, wide),
        out_shape=jax.ShapeDtypeStruct((depth // wide, 2 * rows, wide), mine.dtype),
        in_specs=[SMEM, SMEM] + [ANY] * 6,
        out_specs=VMEM,
        scratch_shapes=[pltpu.SemaphoreType.DMA((3 * NY * NZL,))],
        compiler_params=pltpu.CompilerParams(vmem_limit_bytes=20 * 2**20),
        cost_estimate=pl.CostEstimate(flops=0, bytes_accessed=8 * rows * depth, transcendentals=0),
    )(place, slot, mine, *pieces)


def project_kernel(parts, main, first, last, core_ref, tokens_ref, others_ref, *rest):
    rest = list(rest)
    start_ref = None if first else rest.pop(0)
    cos_ref, sin_ref = (rest.pop(0), rest.pop(0)) if last else (None, None)
    weights, out_ref = rest[: len(parts)], rest[len(parts)]
    acc = rest[len(parts) + 1] if last else out_ref
    two = weights[0].shape[1]
    dim = two // 2
    core = core_ref[0]
    rows = tokens_ref.shape[1]
    acc[...] = jnp.zeros_like(acc) if first else start_ref[...]
    column = pl.multiple_of(core * (main // 2), main // 2)
    for w_ref, part in zip(weights, parts):
        at = 0
        for chunk, begin, n in part:
            i = CHUNKS.index(chunk)
            end = min(begin + n, main)
            for side, ref in enumerate((tokens_ref, others_ref)):
                cut = slice(side * rows, (side + 1) * rows)
                acc[cut, :two] += jnp.dot(
                    ref[i, :, begin:end], w_ref[at : at + end - begin, :], preferred_element_type=jnp.float32
                )
                if begin + n > main:
                    low = at + main - begin
                    packed = w_ref[low : low + main // 4, :]
                    w = jnp.concatenate([packed[:, :dim], packed[:, dim:]], 0)
                    acc[cut, two:] += jnp.dot(
                        ref[i, :, pl.ds(column, main // 2)], w, preferred_element_type=jnp.float32
                    )
            at += n
    if last:
        for h in range(2):
            x = acc[:, h * dim : (h + 1) * dim]
            out = x * cos_ref[...] + pltpu.roll(x, dim // 2, 1) * sin_ref[...]
            out_ref[:, h * dim : (h + 1) * dim] = out.astype(jnp.bfloat16)
        x = acc[:, two:]
        high = x.astype(jnp.bfloat16)
        out_ref[:, two : two + dim] = high
        out_ref[:, two + dim :] = (x - high.astype(jnp.float32)).astype(jnp.bfloat16)


def project(core, tokens, others, weights, parts, main, start, tables):
    rows = 2 * tokens.shape[1]
    cols = weights[0].shape[1]
    first, last = start is None, tables is not None
    extra = ([] if first else [start]) + (list(tables) if last else [])
    taken = sum(w.shape[0] for w in weights)
    acc_shape = (rows, cols + cols // 2)
    return pl.pallas_call(
        functools.partial(project_kernel, parts, main, first, last),
        out_shape=jax.ShapeDtypeStruct((rows, 2 * cols), jnp.bfloat16)
        if last
        else jax.ShapeDtypeStruct(acc_shape, jnp.float32),
        in_specs=[SMEM] + [VMEM] * (2 + len(extra) + len(weights)),
        out_specs=VMEM,
        scratch_shapes=[pltpu.VMEM(acc_shape, jnp.float32)] if last else [],
        compiler_params=pltpu.CompilerParams(vmem_limit_bytes=30 * 2**20),
        cost_estimate=pl.CostEstimate(
            flops=2 * rows * taken * cols, bytes_accessed=2 * taken * (rows + cols), transcendentals=0
        ),
    )(core, tokens, others, *extra, *weights)


def rope_tables(places, head_dim):
    channel = jnp.arange(head_dim // 2).astype(jnp.float32)
    rates = jnp.power(jnp.float32(rope_base), -2.0 * channel / head_dim)
    angles = places[:, None] * rates
    cosine, sine = jnp.cos(angles), jnp.sin(angles)
    return jnp.concatenate([cosine, cosine], -1), jnp.concatenate([-sine, sine], -1)


def sort_rows(perm_ref, x):
    return jnp.dot(perm_ref[...], x, preferred_element_type=jnp.float32).astype(jnp.bfloat16)


def over_cache(block, key_block, bounds_ref, lens_ref, kt_ref, v_ref, qs, scores, put):
    heads, rows, dim = qs.shape
    m_rows = heads * block
    scale = jnp.float32(math.log2(math.e) / math.sqrt(dim))
    tiles = key_block // dim
    count = rows // block

    def score(b, j, peak):
        off = pl.multiple_of(j * key_block, key_block)
        q = qs[:, b * block : (b + 1) * block, :].reshape(m_rows, dim)
        left = lens_ref[b * block : (b + 1) * block, :] - off
        lane = lax.broadcasted_iota(jnp.int32, (block, dim), 1)
        s = jnp.dot(q, kt_ref[:, pl.ds(off, key_block)], preferred_element_type=jnp.float32)
        for t in range(tiles):
            seen = lane < left - t * dim
            tile = jnp.concatenate(
                [
                    jnp.where(seen, s[h * block : (h + 1) * block, t * dim : (t + 1) * dim], -1e30)
                    for h in range(heads)
                ],
                0,
            )
            scores[b % 2, :, pl.ds(off + t * dim, dim)] = tile
            peak = jnp.maximum(peak, tile)
        return peak

    def mix(b, j, shift, sums):
        total, mixed = sums
        off = pl.multiple_of(j * key_block, key_block)
        low_bits = []
        for t in range(tiles):
            w = jnp.exp2(scores[b % 2, :, pl.ds(off + t * dim, dim)] * scale - shift)
            total = total + w
            low_bits.append(w.astype(jnp.bfloat16))
        mixed = mixed + jnp.dot(
            jnp.concatenate(low_bits, 1), v_ref[pl.ds(off, key_block), :], preferred_element_type=jnp.float32
        )
        return total, mixed

    zero = jnp.zeros((m_rows, dim), jnp.float32)
    lowest = jnp.full((m_rows, dim), -1e30, jnp.float32)
    peak, shift, before = None, None, 0
    for b in range(count + 1):
        now = bounds_ref[b] if b < count else 0
        peak_next, sums = lowest, (zero, zero)
        if b == 0:
            peak_next = lax.fori_loop(0, now, lambda j, p: score(0, j, p), peak_next)
        elif b < count:

            def step(j, carry, b=b, shift=shift):
                return score(b, j, carry[0]), mix(b - 1, j, shift, carry[1])

            peak_next, sums = lax.fori_loop(0, before, step, (peak_next, sums))
            peak_next = lax.fori_loop(before, now, lambda j, p, b=b: score(b, j, p), peak_next)
        else:
            sums = lax.fori_loop(0, before, lambda j, s, b=b, shift=shift: mix(b - 1, j, shift, s), sums)
        if b > 0:
            total = jnp.broadcast_to(jnp.sum(sums[0], -1, keepdims=True), (m_rows, dim))
            put((b - 1) * block, peak, total, sums[1])
        if b < count:
            peak = jnp.broadcast_to(jnp.max(peak_next, -1, keepdims=True), (m_rows, dim))
            shift = peak * scale
        before = now


def keep(refs, heads, block):
    def put(r0, *values):
        for ref, value in zip(refs, values):
            ref[:, r0 : r0 + block, :] = value.reshape(heads, block, value.shape[1])

    return put


def early_kernel(block, key_block, bounds_ref, a_ref, b_ref, perm_ref, lens_ref, kt_ref, v_ref, *rest):
    outs, scores = rest[:4], rest[4]
    qs = outs[0]
    dim = qs.shape[2]
    for i, ref in enumerate((a_ref, b_ref)):
        for h in range(2):
            qs[2 * i + h] = sort_rows(perm_ref, ref[:, h * dim : (h + 1) * dim])
    put = keep(outs[1:], 4, block)
    over_cache(block, key_block, bounds_ref, lens_ref, kt_ref, v_ref, qs, scores, put)


def late_kernel(block, key_block, half_ref, column_ref, bounds_ref, *rest):
    parts, early, rest = rest[:4], rest[4:8], rest[8:]
    cos_ref, sin_ref, perm_ref, back_ref, lens_ref, kt_ref, v_ref, out_ref, qs, scores, fresh, result = rest
    dim = qs.shape[2]
    scale = jnp.float32(math.log2(math.e) / math.sqrt(dim))
    for i, ref in enumerate(parts[2:]):
        for h in range(2):
            qs[2 * i + h] = sort_rows(perm_ref, ref[:, h * dim : (h + 1) * dim])
    sums = [
        sum(ref[:, c : c + dim].astype(jnp.float32) for c in range(2 * dim, ref.shape[1], dim)) for ref in parts
    ]
    near, far = sums[0] + sums[1], sums[2] + sums[3]
    first = half_ref[0] == 0
    key = jnp.where(first, near, far)
    key = key * cos_ref[...] + pltpu.roll(key, dim // 2, 1) * sin_ref[...]
    fresh[0] = sort_rows(perm_ref, key.astype(jnp.bfloat16)).astype(jnp.float32)
    fresh[1] = sort_rows(perm_ref, jnp.where(first, far, near).astype(jnp.bfloat16)).astype(jnp.float32)

    def finish(q, cut, peak, total, mixed):
        own = jnp.sum(q.astype(jnp.float32) * fresh[0, cut, :], -1, keepdims=True)
        top = jnp.maximum(peak, own)
        shrink = jnp.exp2((peak - top) * scale)
        own_weight = jnp.exp2((own - top) * scale)
        low = own_weight.astype(jnp.bfloat16).astype(jnp.float32)
        value = mixed * shrink + low * fresh[1, cut, :]
        return (value / (total * shrink + own_weight)).astype(jnp.bfloat16)

    def put(r0, peak, total, mixed):
        cut = slice(r0, r0 + block)
        for h in range(4):
            at = slice(h * block, (h + 1) * block)
            result[4 + h, cut, :] = finish(qs[h, cut, :], cut, peak[at], total[at], mixed[at])
            result[h, cut, :] = finish(*[early[0][h, cut, :], cut] + [ref[h, cut, :] for ref in early[1:]])

    over_cache(block, key_block, bounds_ref, lens_ref, kt_ref, v_ref, qs, scores, put)
    for i in range(4):
        for h in range(2):
            column = pl.multiple_of((column_ref[i] + h) * dim, dim)
            rows_back = jnp.dot(back_ref[...], result[2 * i + h], preferred_element_type=jnp.float32)
            out_ref[:, pl.ds(column, dim)] = rows_back.astype(jnp.bfloat16)


def attention_call(kernel, out_shape, scratch, smem, args, rows, context, dim):
    heads = 4
    many = isinstance(out_shape, list)
    return pl.pallas_call(
        kernel,
        out_shape=out_shape,
        in_specs=[SMEM] * smem + [VMEM] * (len(args) - smem),
        out_specs=[VMEM] * len(out_shape) if many else VMEM,
        scratch_shapes=scratch,
        compiler_params=pltpu.CompilerParams(vmem_limit_bytes=30 * 2**20),
        cost_estimate=pl.CostEstimate(
            flops=4 * heads * rows * context * dim,
            bytes_accessed=4 * context * dim,
            transcendentals=heads * rows * context,
        ),
    )(*args)


def local(tokens, lengths, owner, wq_slabs, wkv_slabs, cache_keys, resident_value_cache):
    mine = tokens[0]
    lens = lengths[0]
    rows, depth = mine.shape
    dim = cache_keys.shape[2]
    part = wq_slabs.shape[1]
    y, zh, co, x, zl = (lax.axis_index(name) for name in AXES)
    z = zh * NZL + zl
    holder = owner[0] % (NY * NZH * NCO)
    y0, zh0, co0 = holder // (NZH * NCO), holder // NCO % NZH, holder % NCO
    main = part // NY
    fifth = main // 4
    chunk = main + fifth
    cut = main * 3 // 4

    wq, wkv = wq_slabs[0], wkv_slabs[0, :, 0]
    from_core = send(pack(1 - co, wq, wkv, main, fifth, dim), other_core)
    held = pack(co, wq, wkv, main, fifth, dim)

    def slab(lo, hi):
        return jnp.where(co == co0, held[lo * chunk : hi * chunk], from_core[lo * chunk : hi * chunk])

    rel = (y - y0) % NY
    up = send(slab(2, 5), y_step(1))
    down = send(slab(5, 8), y_step(-1))

    width = depth // NX
    pair_0 = send(lax.dynamic_slice(mine, (0, x * width), (rows, width)), z_pair)
    other_lens = [send(lengths, to)[0] for to in (z_pair, other_core, z_pair_other_core)]
    pair_up, pair_down = send(pair_0, x_step(1)), send(pair_0, x_step(-1))
    pair_far = [send(pair_up[: rows // 2], x_step(1)), send(pair_down[rows // 2 :], x_step(-1))]

    zs = (z + jnp.array([0, NZ - 2, 2, 4])) % NZ
    quarter = jnp.where(zs // NZL == zh0, zs % NZL, NZL - 1 - zs % NZL)
    rels = (rel + jnp.array([0, NY - 1, 1, 2])) % NY
    place = (quarter[:, None] * NY + rels[None, :]).reshape(-1).astype(jnp.int32)
    turn = (quarter - x) % NX
    slot = jnp.where(turn == 0, 0, jnp.where(turn == 3, 1, jnp.where(turn == 1, 2, 3)))
    slot = jnp.repeat(slot, NY).astype(jnp.int32)

    index = jnp.arange(rows)
    before = (lens[None, :] < lens[:, None]) | ((lens[None, :] == lens[:, None]) & (index[None, :] < index[:, None]))
    rank = jnp.sum(before.astype(jnp.int32), 1)
    hot = rank[None, :] == index[:, None]
    sorted_lens = jnp.sum(jnp.where(hot, lens[None, :], 0), 1)
    perm, back = hot.astype(jnp.bfloat16), hot.T.astype(jnp.bfloat16)
    context = cache_keys.shape[1]
    block, key_block = math.gcd(rows, 64), math.gcd(context, 1024)
    groups = sorted_lens.reshape(rows // block, block)
    bounds = ((groups[:, -1] + key_block - 1) // key_block).astype(jnp.int32)
    lens_wide = jnp.broadcast_to(sorted_lens[:, None], (rows, dim))
    keys_t, values = cache_keys[0].T, resident_value_cache[0]
    odd = z % 2
    columns = jnp.stack(
        [4 * odd + 2 * co, 4 * odd + 2 * (1 - co), 4 * (1 - odd) + 2 * co, 4 * (1 - odd) + 2 * (1 - co)]
    ).astype(jnp.int32)
    cores, odds = co.reshape(1), odd.reshape(1).astype(jnp.int32)
    up, down, place, slot, perm, back, lens_wide, keys_t, bounds, columns, cores, odds = lax.optimization_barrier(
        (up, down, place, slot, perm, back, lens_wide, keys_t, bounds, columns, cores, odds)
    )

    far = send(up[2 * chunk :], y_step(1)), send(down[:chunk], y_step(-1))
    got = [
        jnp.where(
            rel == 0,
            slab(p, p + 1),
            jnp.where(
                rel == 1,
                up[p * chunk : (p + 1) * chunk],
                jnp.where(rel == 2, far[p], down[(p + 1) * chunk : (p + 2) * chunk]),
            ),
        )
        for p in range(2)
    ]
    mirrored = send(jnp.where(odd == 0, got[1], got[0]), z_mirror)
    own = jnp.where(zh == zh0, jnp.where(odd == 0, got[0], got[1]), mirrored)

    n0 = own
    own, pair_0, pair_up, pair_down, pair_far[0], pair_far[1], *other_lens = lax.optimization_barrier(
        (own, pair_0, pair_up, pair_down, *pair_far, *other_lens)
    )
    z_up, z_down = send(own, z_step(2)), send(own, z_step(-2))
    y_up0, y_down0 = send(own, y_step(1)), send(own, y_step(-1))
    here = order_tokens(place, slot, main, mine, [pair_0, pair_up, pair_down] + pair_far)
    z_up, z_down, y_up0, y_down0, here = lax.optimization_barrier((z_up, z_down, y_up0, y_down0, here))
    n1 = jnp.concatenate([z_up, z_down], 0)
    y_up1, y_down1 = send(n1, y_step(1)), send(n1, y_step(-1))
    n2 = send(z_up, z_step(2))
    there = send(here, other_core)

    all_lens = jnp.concatenate([lens] + other_lens)
    cosine, sine = rope_tables(all_lens.astype(jnp.float32), dim)

    y_up1, y_down1, n2, there, cosine, sine = lax.optimization_barrier((y_up1, y_down1, n2, there, cosine, sine))
    y_up2, y_down2 = send(n2, y_step(1)), send(n2, y_step(-1))
    y_far1 = [
        send(jnp.concatenate([y_up0[:cut], y_up1[:chunk]], 0), y_step(1)),
        send(jnp.concatenate([y_down0[cut:], y_down1[chunk:]], 0), y_step(-1)),
    ]
    def whole(c):
        return [(c, 0, chunk)]

    top, bottom = (0, cut), (cut, chunk - cut)
    acc = project(
        cores,
        here,
        there,
        [n0, y_up0, y_down0, n1, y_up1, y_down1],
        [whole(0), whole(1), whole(2)] + [whole(NY + i) + whole(2 * NY + i) for i in range(3)],
        main,
        None,
        None,
    )
    y_up2, y_down2, y_far1, acc = lax.optimization_barrier((y_up2, y_down2, y_far1, acc))
    y_far2 = [send(y_up2[:cut], y_step(1)), send(y_down2[cut:], y_step(-1))]
    acc = project(
        cores,
        here,
        there,
        y_far1 + [n2, y_up2, y_down2],
        [[(3,) + top] + whole(NY + 3), [(3,) + bottom] + whole(2 * NY + 3)] + [whole(3 * NY + i) for i in range(3)],
        main,
        acc,
        None,
    )
    out = project(
        cores,
        here,
        there,
        y_far2,
        [[(3 * NY + 3,) + top], [(3 * NY + 3,) + bottom]],
        main,
        acc,
        (cosine, sine),
    )
    near = [out[:rows], send(out[2 * rows : 3 * rows], other_core)]
    far = [
        send(out[rows : 2 * rows, : 3 * dim], z_pair),
        send(out[3 * rows :, : 3 * dim], z_pair_other_core),
    ]

    four = (4, rows, dim)
    scores = pltpu.VMEM((2, 4 * block, context), jnp.float32)
    early = attention_call(
        functools.partial(early_kernel, block, key_block),
        [jax.ShapeDtypeStruct(four, jnp.bfloat16)] + [jax.ShapeDtypeStruct(four, jnp.float32)] * 3,
        [scores],
        1,
        (bounds, *near, perm, lens_wide, keys_t, values),
        rows, context, dim,
    )
    result = attention_call(
        functools.partial(late_kernel, block, key_block),
        jax.ShapeDtypeStruct((rows, 8 * dim), jnp.bfloat16),
        [
            pltpu.VMEM(four, jnp.bfloat16),
            scores,
            pltpu.VMEM((2, rows, dim), jnp.float32),
            pltpu.VMEM((8, rows, dim), jnp.bfloat16),
        ],
        3,
        (odds, columns, bounds, *near, *far, *early)
        + (cosine[:rows], sine[:rows], perm, back, lens_wide, keys_t, values),
        rows, context, dim,
    )
    return result[None]


def solution(mesh):
    fine = Mesh(mesh.devices.reshape(NY, NZH, NCO, NX, NZL), AXES)
    layer = ("y", "z_hi", "core")
    return jax.shard_map(
        local,
        mesh=fine,
        in_specs=(
            P("dp", layer, None),
            P("dp", layer),
            P(),
            P(layer, "dp", "head"),
            P(layer, "dp", "head", None),
            P("dp", None, "head"),
            P("dp", None, "head"),
        ),
        out_specs=P("dp", layer, "head"),
        check_vma=False,
    )
```
